512 devices in a mesh: leaf: 32 (over z, x), front: 16 (over y, core).
Axes of the slice: x: 4, y: 8, z: 8, core: 2. Of those that a mesh axis runs over, the one named last changes fastest.
Arguments:
- rhs_child: float32 [32, 128, 2048], P('leaf', None, 'front'), may hold values from -8 to 8
- child_inverse: float32 [32, 2048, 2048], P('leaf', 'front'), as said below
- update_block: float32 [32, 1024, 2048], P('leaf', None, 'front'), may hold values from -0.125 to 0.125
- row_map: int32 [32, 1024], P('leaf'), may hold values from 0 to 8191, as said below
- rhs_root: float32 [128, 8192], P('front', 'leaf'), may hold values from -8 to 8
- root_inverse: float32 [8192, 8192], P('front', 'leaf'), as said below
Outputs:
- child_solution: float32 [32, 128, 2048], P('leaf', None, 'front')
- root_solution: float32 [128, 8192], P('front', 'leaf')
The draws below stay inside these ranges and needn't reach their ends.
Inputs may be any that keep to these rules, and one draw needn't show every extreme that they name: `row_map`: each row holds 1024 distinct root rows, and every row names both 0 and 8191. `child_inverse`: each matrix is lower triangular with a positive diagonal. `root_inverse`: lower triangular with a positive diagonal.
All inputs are finite; a program needn't handle non-finite values.
Results may differ from the reference program's by a relative error of at most 0.000075.
Values sent between devices are 32-bit elements; how exact they have to be, the bound alone decides.
A program may use at most 64 MiB of HBM per device.

```python
import math
import jax
import jax.numpy as jnp
from jax import lax

P_SIZE = 8192
C = 2048
U = 1024
R = 128
SUBTREES = 32


def triangle(offdiag, diagonal):
    shape = offdiag.shape
    rows = lax.broadcasted_iota(jnp.int32, shape, len(shape) - 2)
    cols = lax.broadcasted_iota(jnp.int32, shape, len(shape) - 1)
    lower = jnp.where(rows > cols, offdiag, 0.0)
    return lower + jnp.where(rows == cols, diagonal, 0.0)


def draw_child_inverse(key, part):
    key = jax.random.fold_in(key, 11)
    key_off, key_diag = jax.random.split(key, 2)
    shape = (SUBTREES, C, C)
    offdiag = jax.random.normal(key_off, shape, jnp.float32) * (0.8 / math.sqrt(C))
    diagonal = jnp.exp(jax.random.uniform(key_diag, (SUBTREES, C, 1), jnp.float32, math.log(0.5), math.log(2.0)))
    return triangle(offdiag, diagonal)


def draw_root_inverse(key, part):
    key = jax.random.fold_in(key, 13)
    key_off, key_diag = jax.random.split(key, 2)
    shape = (P_SIZE, P_SIZE)
    offdiag = jax.random.normal(key_off, shape, jnp.float32) * (0.8 / math.sqrt(P_SIZE))
    diagonal = jnp.exp(jax.random.uniform(key_diag, (P_SIZE, 1), jnp.float32, math.log(0.5), math.log(2.0)))
    return triangle(offdiag, diagonal)


def draw_row_map(key, part):
    key = jax.random.fold_in(key, 17)
    scores = jax.random.randint(key, (SUBTREES, P_SIZE), 2, 2 ** 30)
    places = lax.broadcasted_iota(jnp.int32, (SUBTREES, P_SIZE), 1)
    scores = jnp.where(places == P_SIZE - 1, 0, scores)
    scores = jnp.where(places == 0, 1, scores)
    ordering = jnp.argsort(scores, axis=1, stable=True)
    return ordering[:, :U].astype(jnp.int32)


def level_of(key, extent, shards, smallest, largest):
    loudness, own = 1.0, jax.random.fold_in(key, 6)
    for axis_at, blocks in shards:
        heights = jnp.exp(jax.random.uniform(jax.random.fold_in(own, axis_at), (blocks,), jnp.float32, smallest / len(shards), largest / len(shards)))
        loudness = loudness * jnp.repeat(heights, extent[axis_at] // blocks).reshape([-1 if axis == axis_at else 1 for axis in range(len(extent))])
    return loudness


def noise(stream_key, extent, spread, most, cuts=(), kind=jnp.bfloat16):
    result = jax.random.normal(stream_key, extent, jnp.float32) * spread
    if len(cuts) > 0:
        result = level_of(stream_key, extent, cuts, -0.22, 0.18) * result
    return jnp.clip(result, min=-most, max=most).astype(kind)


def setup_inputs(seed: int = 0) -> dict:
    streams_of = jax.random.split(jax.random.key(seed), 7)
    return {
        "rhs_child": noise(streams_of[0], (SUBTREES, R, C), 1.0, 8.0, ((0, 32), (2, 16)), jnp.float32),
        "child_inverse": draw_child_inverse(jax.random.fold_in(streams_of[6], 71), 0),
        "update_block": noise(streams_of[2], (SUBTREES, U, C), C ** -0.5, 0.125, ((0, 32), (2, 16)), jnp.float32),
        "row_map": draw_row_map(jax.random.fold_in(streams_of[6], 71), 0),
        "rhs_root": noise(streams_of[4], (R, P_SIZE), 1.0, 8.0, ((0, 16), (1, 32)), jnp.float32),
        "root_inverse": draw_root_inverse(jax.random.fold_in(streams_of[6], 71), 0),
    }


def product(left, right):
    return jnp.dot(left, right, precision=lax.Precision.HIGHEST, preferred_element_type=jnp.float32)


def times_transposed(left, right):
    return lax.dot_general(left, right, (((1,), (1,)), ((), ())), precision=lax.Precision.HIGHEST, preferred_element_type=jnp.float32)


def reference(rhs_child, child_inverse, update_block, row_map, rhs_root, root_inverse):
    def forward_child(items):
        rhs_rows, inverse_rows, update_rows = items
        solved = times_transposed(rhs_rows, inverse_rows)
        return solved, times_transposed(solved, update_rows)

    solved_child, updates = lax.map(forward_child, (rhs_child, child_inverse, update_block))
    flat_updates = jnp.transpose(updates, (1, 0, 2)).reshape(updates.shape[1], -1)
    flat_map = row_map.reshape(-1)
    gathered_sum = jnp.zeros(rhs_root.shape, jnp.float32).at[:, flat_map].add(flat_updates)
    reduced = rhs_root - gathered_sum
    solved_root = times_transposed(reduced, root_inverse)
    root_solution = product(solved_root, root_inverse)
    picked = jnp.transpose(jnp.take(root_solution, row_map, axis=1), (1, 0, 2))

    def backward_child(items):
        solved, picked_rows, update_rows, inverse_rows = items
        return product(solved - product(picked_rows, update_rows), inverse_rows)

    child_solution = lax.map(backward_child, (solved_child, picked, update_block, child_inverse))
    return child_solution, root_solution
```

```python
import functools

import jax
import jax.numpy as jnp
from jax import lax
from jax.experimental import pallas as pl
from jax.experimental.pallas import tpu as pltpu
from jax.sharding import PartitionSpec as P

MESH = pl.DeviceIdType.MESH
F32 = jnp.float32
BF16 = jnp.bfloat16
NN = (((1,), (0,)), ((), ()))
NT = (((1,), (1,)), ((), ()))


def split2(x):
    hi = x.astype(BF16)
    return hi, (x - hi.astype(F32)).astype(BF16)


def split3(x):
    hi = x.astype(BF16)
    rest = x - hi.astype(F32)
    mid = rest.astype(BF16)
    return hi, mid, (rest - mid.astype(F32)).astype(BF16)


def mul(a, b, dims):
    return lax.dot_general(a, b, dims, preferred_element_type=F32)


def mul3(a, bh, bl, dims):
    ah, al = split2(a)
    return mul(ah, bh, dims) + (mul(ah, bl, dims) + mul(al, bh, dims))


def kernel(
    nl, nf,
    rhs_c, inv, upd, rmap, rhs_r, rinv,
    child_out, root_out,
    gath, inv_h, inv_l, upd_h, upd_l, rinv_h, rinv_l, onehot, solved,
    b_send, b_pair, b_own, b_recv,
    c_send, c_recv, d_buf, e_send, e_recv, f_buf, g_send, g_recv, h_buf, i_buf,
    j_send, j_pair, j_own, j_recv,
    s_sem, r_sem, fs_sem, fr_sem, is_sem, ir_sem,
):
    ny, nh = nf // 2, nl // nf
    l = lax.axis_index("leaf")
    f = lax.axis_index("front")
    y, c = f // 2, f % 2
    sib = y * 2 + (1 - c)
    rows, width = rhs_r.shape
    frames = rows * nf
    ks, ku = rhs_c.shape[1], upd.shape[0]

    barrier = pltpu.get_barrier_semaphore()
    for d in range(1, nf):
        pl.semaphore_signal(barrier, inc=1, device_id={"front": (f + d) % nf}, device_id_type=MESH)
    for d in range(1, nl):
        pl.semaphore_signal(barrier, inc=1, device_id={"leaf": (l + d) % nl}, device_id_type=MESH)
    pl.semaphore_wait(barrier, nf + nl - 2)

    pending = []

    def send(src, dst, ss, rs, where):
        copy = pltpu.make_async_remote_copy(
            src_ref=src, dst_ref=dst, send_sem=ss, recv_sem=rs, device_id=where, device_id_type=MESH
        )
        copy.start()
        return copy

    def spread(count, axis, me, src, dst, k):
        for d in range(1, count):
            at = (me + d) % count
            send(src(at), dst(d), s_sem.at[k], r_sem.at[k], {axis: at})

    def wait_recv(ref, sem):
        pltpu.make_async_remote_copy(
            src_ref=ref, dst_ref=ref, send_sem=sem, recv_sem=sem, device_id={"front": sib}, device_id_type=MESH
        ).wait_recv()

    def wait_send(ref, sem):
        pltpu.make_async_remote_copy(
            src_ref=ref, dst_ref=ref, send_sem=sem, recv_sem=sem, device_id={"front": sib}, device_id_type=MESH
        ).wait_send()

    def finish():
        for ref, sem in pending:
            wait_send(ref, sem)

    send(rhs_c, gath.at[f], fs_sem.at[0], fr_sem.at[0], {"front": sib})
    pending.append((rhs_c, fs_sem.at[0]))
    for d in range(1, ny):
        at = ((y + d) % ny) * 2 + c
        send(rhs_c, gath.at[f], is_sem.at[d - 1], ir_sem.at[d - 1], {"front": at})
        pending.append((rhs_c, is_sem.at[d - 1]))
    gath[f] = rhs_c[...]
    for k in range(2):
        part = jnp.concatenate([inv[:, (2 * j + k) * ks : (2 * j + k + 1) * ks] for j in range(ny)], axis=1)
        inv_h[k], inv_l[k] = split2(part)
    upd_h[...], upd_l[...] = split2(upd[...])
    rinv_h[...], rinv_l[...] = split2(rinv[...])
    target = rmap[...]
    low = target % width
    high = target // width
    onehot[...] = jnp.where(lax.broadcasted_iota(jnp.int32, (width, ku), 0) == low, 1.0, 0.0).astype(BF16)
    pick_mask = lambda: lax.broadcasted_iota(jnp.int32, (nl, rows, ku), 0) == high[None]

    for d in range(1, ny):
        came = ((y + ny - d) % ny) * 2 + c
        wait_recv(gath.at[came], ir_sem.at[d - 1])
        send(gath.at[came], gath.at[came], fs_sem.at[d], fr_sem.at[d], {"front": sib})
        pending.append((gath.at[came], fs_sem.at[d]))
    for d in range(ny):
        wait_recv(gath.at[0], fr_sem.at[d])
    total = None
    for k in range(2):
        part = mul3(jnp.concatenate([gath[2 * j + k] for j in range(ny)], axis=1), inv_h[k], inv_l[k], NT)
        total = part if total is None else total + part
    by_core = total.reshape(ny, 2, rows, ks)
    for k in range(2):
        solved[k] = by_core[:, k].reshape(ny * rows, ks)

    b_send[...] = mul3(solved[1 - c], upd_h[...], upd_l[...], NT).reshape(ny, rows, ku)
    send(b_send, b_pair, s_sem.at[0], r_sem.at[0], {"front": sib})
    pending.append((b_send, s_sem.at[0]))
    mine = mul3(solved[c], upd_h[...], upd_l[...], NT).reshape(ny, rows, ku)
    wait_recv(b_pair, r_sem.at[0])
    b_own[...] = mine + b_pair[...]
    for d in range(1, ny):
        at = (y + d) % ny
        send(b_own.at[at], b_recv.at[d - 1], s_sem.at[1], r_sem.at[1], {"front": at * 2 + c})
    pending.append((b_recv, s_sem.at[1]))
    wait_recv(b_recv, r_sem.at[1])
    update = b_own[y] + jnp.sum(b_recv[...], axis=0)

    mask = pick_mask()
    parts = [
        jnp.where(mask, jnp.broadcast_to(p.astype(F32)[None], (nl, rows, ku)), 0.0).reshape(nl * rows, ku).astype(BF16)
        for p in split3(update)
    ]
    c_send[...] = (
        mul(parts[0], onehot[...], NT) + (mul(parts[1], onehot[...], NT) + mul(parts[2], onehot[...], NT))
    ).reshape(nl, rows, width)
    spread(nl, "leaf", l, lambda at: c_send.at[at], lambda d: c_recv.at[d - 1], 2)
    pending.append((c_recv, s_sem.at[2]))
    wait_recv(c_recv, r_sem.at[2])
    reduced = rhs_r[...] - (c_send[l] + jnp.sum(c_recv[...], axis=0))

    d_buf[f] = reduced
    spread(nf, "front", f, lambda at: d_buf.at[f], lambda d: d_buf.at[f], 3)
    pending.append((d_buf.at[pl.ds(0, nf - 1)], s_sem.at[3]))
    wait_recv(d_buf.at[pl.ds(0, nf - 1)], r_sem.at[3])

    part = mul3(d_buf[...].reshape(frames, width), rinv_h[...], rinv_l[...], NT)
    for h in range(nh):
        e_send[h] = part[:, h * width : (h + 1) * width].reshape(nf, rows, width)
    spread(nl, "leaf", l, lambda at: e_send.at[at % nh, at // nh], lambda d: e_recv.at[d - 1], 4)
    pending.append((e_recv, s_sem.at[4]))
    wait_recv(e_recv, r_sem.at[4])
    place = (l % nh) * nf + l // nh
    f_buf[place] = e_send[l % nh, l // nh] + jnp.sum(e_recv[...], axis=0)

    spread(nl, "leaf", l, lambda at: f_buf.at[place], lambda d: f_buf.at[place], 5)
    pending.append((f_buf.at[pl.ds(0, nl - 1)], s_sem.at[5]))
    wait_recv(f_buf.at[pl.ds(0, nl - 1)], r_sem.at[5])
    root = jnp.concatenate([f_buf[h * nf : (h + 1) * nf].reshape(frames, width) for h in range(nh)], axis=1)

    g_send[...] = mul3(root, rinv_h[...], rinv_l[...], NN).reshape(nf, rows, width)
    spread(nf, "front", f, lambda at: g_send.at[at], lambda d: g_recv.at[d - 1], 6)
    pending.append((g_recv, s_sem.at[6]))
    wait_recv(g_recv, r_sem.at[6])
    answer = g_send[f] + jnp.sum(g_recv[...], axis=0)
    h_buf[l] = answer

    spread(nl, "leaf", l, lambda at: h_buf.at[l], lambda d: h_buf.at[l], 7)
    pending.append((h_buf.at[pl.ds(0, nl - 1)], s_sem.at[7]))
    root_out[...] = answer
    wait_recv(h_buf.at[pl.ds(0, nl - 1)], r_sem.at[7])
    hh, hm, hl = split3(h_buf[...].reshape(nl * rows, width))
    chosen = mul(hh, onehot[...], NN) + (mul(hm, onehot[...], NN) + mul(hl, onehot[...], NN))
    picked = jnp.sum(jnp.where(pick_mask(), chosen.reshape(nl, rows, ku), 0.0), axis=0)

    i_buf[f] = picked
    send(i_buf.at[f], i_buf.at[f], fs_sem.at[ny], fr_sem.at[ny], {"front": sib})
    pending.append((i_buf.at[f], fs_sem.at[ny]))
    for d in range(1, ny):
        at = ((y + d) % ny) * 2 + c
        send(i_buf.at[f], i_buf.at[f], is_sem.at[ny - 1 + d - 1], ir_sem.at[ny - 1 + d - 1], {"front": at})
        pending.append((i_buf.at[f], is_sem.at[ny - 1 + d - 1]))
    for d in range(1, ny):
        came = ((y + ny - d) % ny) * 2 + c
        wait_recv(i_buf.at[came], ir_sem.at[ny - 1 + d - 1])
        send(i_buf.at[came], i_buf.at[came], fs_sem.at[ny + d], fr_sem.at[ny + d], {"front": sib})
        pending.append((i_buf.at[came], fs_sem.at[ny + d]))
    for d in range(ny):
        wait_recv(i_buf.at[0], fr_sem.at[ny + d])
    taken = mul3(i_buf[...].reshape(frames, ku), upd_h[...], upd_l[...], NN)
    first = [solved[k].reshape(ny, rows, ks) for k in range(2)]
    before = jnp.stack(first, axis=1).reshape(frames, ks)
    residue = before - taken

    for k in range(2):
        @pl.when(c == 1 - k)
        def _():
            other = mul3(residue, inv_h[k], inv_l[k], NN)
            for j in range(ny):
                j_send[j] = other[:, j * ks : (j + 1) * ks]
    send(j_send, j_pair, s_sem.at[8], r_sem.at[8], {"front": sib})
    pending.append((j_send, s_sem.at[8]))
    mine = mul3(residue, inv_h[c], inv_l[c], NN)
    wait_recv(j_pair, r_sem.at[8])
    for j in range(ny):
        j_own[j] = mine[:, j * ks : (j + 1) * ks] + j_pair[j]
    for d in range(1, ny):
        at = (y + d) % ny
        send(j_own.at[at], j_recv.at[d - 1], s_sem.at[9], r_sem.at[9], {"front": at * 2 + c})
    pending.append((j_recv, s_sem.at[9]))
    wait_recv(j_recv, r_sem.at[9])
    child_out[...] = j_own[y] + jnp.sum(j_recv[...], axis=0)
    finish()


def body(nl, nf, rhs_child, child_inverse, update_block, row_map, rhs_root, root_inverse):
    ny = nf // 2
    frames, ks = rhs_child.shape[1:]
    ku = update_block.shape[1]
    rows, width = rhs_root.shape
    deep = root_inverse.shape[0]
    vm = pltpu.VMEM
    scratch = [
        vm((nf, frames, ks), F32),
        vm((2, ks, ny * ks), BF16), vm((2, ks, ny * ks), BF16),
        vm((ku, ks), BF16), vm((ku, ks), BF16),
        vm((deep, width), BF16), vm((deep, width), BF16),
        vm((width, ku), BF16),
        vm((2, ny * rows, ks), F32),
        vm((ny, rows, ku), F32), vm((ny, rows, ku), F32), vm((ny, rows, ku), F32), vm((ny - 1, rows, ku), F32),
        vm((nl, rows, width), F32), vm((nl - 1, rows, width), F32),
        vm((nf, rows, width), F32),
        vm((nl // nf, nf, rows, width), F32), vm((nl - 1, rows, width), F32),
        vm((nl, rows, width), F32),
        vm((nf, rows, width), F32), vm((nf - 1, rows, width), F32),
        vm((nl, rows, width), F32),
        vm((nf, rows, ku), F32),
        vm((ny, frames, ks), F32), vm((ny, frames, ks), F32), vm((ny, frames, ks), F32), vm((ny - 1, frames, ks), F32),
        pltpu.SemaphoreType.DMA((10,)), pltpu.SemaphoreType.DMA((10,)),
        pltpu.SemaphoreType.DMA((2 * ny,)), pltpu.SemaphoreType.DMA((2 * ny,)),
        pltpu.SemaphoreType.DMA((2 * ny - 2,)), pltpu.SemaphoreType.DMA((2 * ny - 2,)),
    ]
    child, root = pl.pallas_call(
        functools.partial(kernel, nl, nf),
        out_shape=(
            jax.ShapeDtypeStruct((frames, ks), F32),
            jax.ShapeDtypeStruct((rows, width), F32),
        ),
        in_specs=[pl.BlockSpec(memory_space=pltpu.VMEM)] * 6,
        out_specs=(pl.BlockSpec(memory_space=pltpu.VMEM),) * 2,
        scratch_shapes=scratch,
        compiler_params=pltpu.CompilerParams(
            collective_id=0, has_side_effects=True, vmem_limit_bytes=48 * 1024 * 1024
        ),
    )(rhs_child[0], child_inverse[0], update_block[0], row_map, rhs_root, root_inverse)
    return child[None], root


def solution(mesh):
    placed = (
        P("leaf", None, "front"),
        P("leaf", "front", None),
        P("leaf", None, "front"),
        P("leaf", None),
        P("front", "leaf"),
        P("front", "leaf"),
    )
    return jax.shard_map(
        functools.partial(body, mesh.shape["leaf"], mesh.shape["front"]),
        mesh=mesh,
        in_specs=placed,
        out_specs=(P("leaf", None, "front"), P("front", "leaf")),
        check_vma=False,
    )
```

```python
import functools

import jax
import jax.numpy as jnp
from jax import lax
from jax.experimental import pallas as pl
from jax.experimental.pallas import tpu as pltpu
from jax.sharding import PartitionSpec as P

NX = 4
MESH = pl.DeviceIdType.MESH
F32 = jnp.float32
BF16 = jnp.bfloat16
NN = (((1,), (0,)), ((), ()))
NT = (((1,), (1,)), ((), ()))


def split2(x):
    hi = x.astype(BF16)
    return hi, (x - hi.astype(F32)).astype(BF16)


def split3(x):
    hi = x.astype(BF16)
    rest = x - hi.astype(F32)
    mid = rest.astype(BF16)
    return hi, mid, (rest - mid.astype(F32)).astype(BF16)


def mul(a, b, dims):
    return lax.dot_general(a, b, dims, preferred_element_type=F32)


def mul3(a, bh, bl, dims):
    ah, al = split2(a)
    return mul(ah, bh, dims) + (mul(ah, bl, dims) + mul(al, bh, dims))


def ring_hops(d, n):
    return min(d, n - d)


def kernel(
    nl, nf,
    rhs_c, inv, upd, rmap, rhs_r, rinv,
    child_out, root_out,
    rhs_v, inv_v, upd_v, rinv_v, map_v, rr_v,
    gath, acc, inv_h, inv_l, upd_h, upd_l, rinv_h, rinv_l, onehot,
    b_send, b_pair, b_own, b_recv, c_send, c_recv, d_buf, e_send, e_recv, f_buf,
    g_send, g_recv, h_buf, i_buf, j_send, j_pair, j_own, j_recv,
    in_sem, a_ss, a_rs, af_ss, af_rs, i_ss, i_rs, if_ss, if_rs, s_sem, r_sem, g_ss, j_ss, j_rs,
):
    ny = nf // 2
    nz = nl // NX
    l = lax.axis_index("leaf")
    f = lax.axis_index("front")
    y, c = f // 2, f % 2
    z, x = l // NX, l % NX
    sib = y * 2 + (1 - c)
    rows, width = rr_v.shape
    ks, ku = acc.shape[2], upd_v.shape[0]
    half = ny * rows
    piece = e_recv.shape[-1]
    nq = e_send.shape[1]

    far_y = sorted(range(1, ny), key=lambda d: -ring_hops(d, ny))
    near_y = sorted(range(1, ny), key=lambda d: ring_hops(d, ny))
    far_l = sorted(
        [(dz, dx) for dz in range(nz) for dx in range(NX) if dz or dx],
        key=lambda d: -(ring_hops(d[0], nz) + ring_hops(d[1], NX)),
    )

    loads = [
        pltpu.make_async_copy(src, dst, in_sem.at[k])
        for k, (src, dst) in enumerate(
            [(rhs_c, rhs_v), (inv, inv_v), (upd, upd_v), (rmap, map_v), (rinv, rinv_v), (rhs_r, rr_v)]
        )
    ]
    for load in loads:
        load.start()
    barrier = pltpu.get_barrier_semaphore()
    for d in range(1, nf):
        pl.semaphore_signal(barrier, inc=1, device_id={"front": (f + d) % nf}, device_id_type=MESH)
    for d in range(1, nl):
        pl.semaphore_signal(barrier, inc=1, device_id={"leaf": (l + d) % nl}, device_id_type=MESH)
    loads[0].wait()
    pl.semaphore_wait(barrier, nf + nl - 2)

    pending = []

    def send(src, dst, ss, rs, where, when=None):
        pltpu.make_async_remote_copy(
            src_ref=src, dst_ref=dst, send_sem=ss, recv_sem=rs, device_id=where, device_id_type=MESH
        ).start()

    def both(ref, sem):
        return pltpu.make_async_remote_copy(
            src_ref=ref, dst_ref=ref, send_sem=sem, recv_sem=sem, device_id={"front": sib}, device_id_type=MESH
        )

    def wait_recv(ref, sem):
        both(ref, sem).wait_recv()

    def sent(ref, sem, when=None):
        pending.append((ref, sem, when))

    def finish():
        for ref, sem, when in pending:
            if when is None:
                both(ref, sem).wait_send()
            else:
                @pl.when(when)
                def _():
                    both(ref, sem).wait_send()

    def on_leaf(k, src, dst, ss, rs):
        for n, (dz, dx) in enumerate(far_l):
            at_z, at_x = (z + dz) % nz, (x + dx) % NX
            send(src(at_z, at_x), dst(n), ss, rs, {"leaf": at_z * NX + at_x})

    for h in range(2):
        send(rhs_v.at[:, h], gath.at[h, f], af_ss.at[h, 0], af_rs.at[h, 0], {"front": sib})
        sent(rhs_v.at[:, h], af_ss.at[h, 0])
        for d in far_y:
            up = y + d < ny

            @pl.when(up)
            def _():
                send(
                    rhs_v.at[:, h], gath.at[h, f], a_ss.at[h, d], a_rs.at[h, d], {"front": (y + d) % ny * 2 + c}
                )

            sent(rhs_v.at[:, h], a_ss.at[h, d], up)
    for h in range(2):
        gath[h, f] = rhs_v[:, h]

    loads[1].wait()
    for j in range(ny):
        inv_h[j], inv_l[j] = split2(inv_v[:, 2 * j * ks : 2 * (j + 1) * ks])
    loads[2].wait()
    upd_h[...], upd_l[...] = split2(upd_v[...])
    loads[3].wait()
    low = map_v[...] % width
    onehot[...] = jnp.where(lax.broadcasted_iota(jnp.int32, (width, ku), 0) == low, 1.0, 0.0).astype(BF16)

    def in_block():
        return lax.broadcasted_iota(jnp.int32, (nl, rows, ku), 0) == (map_v[...] // width)[None]

    def solve_step(h, at):
        pair = jnp.concatenate([gath[h, 2 * at + k].reshape(half, ks) for k in range(2)], axis=1)
        return mul3(pair, inv_h[at], inv_l[at], NT)

    def solve(h):
        def step(d):
            wait_recv(gath.at[h, 0], af_rs.at[h, d])
            acc[h] += solve_step(h, (y + ny - d) % ny)

        wait_recv(gath.at[h, 0], af_rs.at[h, 0])
        acc[h] = solve_step(h, y)
        before = None
        for d in near_y:
            low_chip = y >= d

            @pl.when(low_chip)
            def _():
                came = (y + ny - d) % ny * 2 + c
                wait_recv(gath.at[h, came], a_rs.at[h, d])
                send(gath.at[h, came], gath.at[h, came], af_ss.at[h, d], af_rs.at[h, d], {"front": sib})

            sent(gath.at[h, 0], af_ss.at[h, d], low_chip)
            if before is not None:
                @pl.when(y >= before)
                def _():
                    step(before)
            before = d

        @pl.when(y >= before)
        def _():
            step(before)

    def partial_update(h):
        return mul3(acc[h], upd_h[...], upd_l[...], NT).reshape(ny, rows, ku)

    def give_update(h):
        @pl.when(c != h)
        def _():
            b_send[...] = partial_update(h)
            send(b_send, b_pair, s_sem.at[0], r_sem.at[0], {"front": sib})

        @pl.when(c == h)
        def _():
            mine = partial_update(h)
            wait_recv(b_pair, r_sem.at[0])
            b_own[...] = mine + b_pair[...]
            for n, d in enumerate(far_y):
                at = (y + d) % ny
                send(b_own.at[at], b_recv.at[n], s_sem.at[1], r_sem.at[1], {"front": at * 2 + c})

    sent(b_send, s_sem.at[0])
    sent(b_recv, s_sem.at[1])

    def give_columns():
        wait_recv(b_recv, r_sem.at[1])
        update = b_own[y] + jnp.sum(b_recv[...], axis=0)
        mask = in_block()
        parts = [
            jnp.where(mask, jnp.broadcast_to(p.astype(F32)[None], (nl, rows, ku)), 0.0)
            .reshape(nl * rows, ku)
            .astype(BF16)
            for p in split3(update)
        ]
        c_send[...] = (
            mul(parts[0], onehot[...], NT) + (mul(parts[1], onehot[...], NT) + mul(parts[2], onehot[...], NT))
        ).reshape(nl, rows, width)
        on_leaf(2, lambda at_z, at_x: c_send.at[at_z * NX + at_x], lambda n: c_recv.at[n], s_sem.at[2], r_sem.at[2])

    sent(c_recv, s_sem.at[2])

    def give_reduced(h):
        wait_recv(c_recv, r_sem.at[2])
        d_buf[h, y] = rr_v[...] - (c_send[l] + jnp.sum(c_recv[...], axis=0))
        for d in far_y:
            for k in range(2):
                at = (y + d) % ny * 2 + k
                send(d_buf.at[h, y], d_buf.at[h, y], s_sem.at[3], r_sem.at[3 + h], {"front": at})
        send(d_buf.at[h, y], d_buf.at[h, y], s_sem.at[3], r_sem.at[3 + h], {"front": sib})

    sent(c_recv.at[pl.ds(0, nf - 1)], s_sem.at[3])

    def give_forward(h):
        @pl.when(c == h)
        def _():
            wait_recv(d_buf.at[h, pl.ds(0, ny - 1)], r_sem.at[3 + h])

        @pl.when(c != h)
        def _():
            wait_recv(d_buf.at[h], r_sem.at[3 + h])

        part = mul3(d_buf[h].reshape(half, width), rinv_h[...], rinv_l[...], NT)
        for q in range(nq):
            e_send[h, q] = part[:, q * piece : (q + 1) * piece].reshape(ny, rows, piece)
        on_leaf(
            5 + h, lambda at_z, at_x: e_send.at[h, at_x, at_z], lambda n: e_recv.at[h, n], s_sem.at[5 + h], r_sem.at[5 + h]
        )

    def give_solved(h):
        wait_recv(e_recv.at[h], r_sem.at[5 + h])
        f_buf[h, x, z] = e_send[h, x, z] + jnp.sum(e_recv[h], axis=0)
        on_leaf(
            7 + h, lambda at_z, at_x: f_buf.at[h, x, z], lambda n: f_buf.at[h, x, z], s_sem.at[7 + h], r_sem.at[7 + h]
        )

    for h in range(2):
        sent(e_recv.at[h], s_sem.at[5 + h])
        sent(e_recv.at[h], s_sem.at[7 + h])

    def give_backward(h):
        wait_recv(e_recv.at[h], r_sem.at[7 + h])
        root = jnp.concatenate([f_buf[h, q].reshape(half, piece) for q in range(nq)], axis=1)
        g_send[h] = mul3(root, rinv_h[...], rinv_l[...], NN).reshape(ny, rows, width)
        for d in far_y:
            at = (y + d) % ny
            send(g_send.at[h, at], g_recv.at[f], g_ss.at[h, 0], r_sem.at[9], {"front": at * 2 + h})

        @pl.when(c != h)
        def _():
            send(g_send.at[h, y], g_recv.at[f], g_ss.at[h, 1], r_sem.at[9], {"front": sib})

        @pl.when(c == h)
        def _():
            g_recv[f] = g_send[h, y]

        sent(g_send.at[h, pl.ds(0, ny - 1)], g_ss.at[h, 0])
        sent(g_send.at[h, 0], g_ss.at[h, 1], c != h)

    def give_root():
        wait_recv(g_recv.at[pl.ds(0, nf - 1)], r_sem.at[9])
        answer = jnp.sum(g_recv[...], axis=0)
        h_buf[l] = answer
        on_leaf(9, lambda at_z, at_x: h_buf.at[l], lambda n: h_buf.at[l], s_sem.at[9], r_sem.at[10])
        root_out[...] = answer

    sent(h_buf.at[pl.ds(0, nl - 1)], s_sem.at[9])

    def give_picked(h):
        wait_recv(h_buf.at[pl.ds(0, nl - 1)], r_sem.at[10])
        parts = split3(h_buf[...].reshape(nl * rows, width))
        chosen = mul(parts[0], onehot[...], NN) + (mul(parts[1], onehot[...], NN) + mul(parts[2], onehot[...], NN))
        i_buf[h, y] = jnp.sum(jnp.where(in_block(), chosen.reshape(nl, rows, ku), 0.0), axis=0)
        for d in far_y:
            at = (y + d) % ny * 2 + c
            send(i_buf.at[h, y], i_buf.at[h, y], i_ss.at[d], i_rs.at[d], {"front": at})
        send(i_buf.at[h, y], i_buf.at[h, y], if_ss.at[0], if_rs.at[0], {"front": sib})

    for d in range(ny):
        if d:
            sent(i_buf.at[0, 0], i_ss.at[d])
        sent(i_buf.at[0, 0], if_ss.at[d])

    def take_picked(h):
        @pl.when(c == h)
        def _():
            for d in near_y:
                came = (y + ny - d) % ny
                wait_recv(i_buf.at[h, came], i_rs.at[d])
                send(i_buf.at[h, came], i_buf.at[h, came], if_ss.at[d], if_rs.at[d], {"front": sib})

        @pl.when(c != h)
        def _():
            for d in range(ny):
                wait_recv(i_buf.at[h, 0], if_rs.at[d])

    def give_residue(h):
        residue = acc[h] - mul3(i_buf[h].reshape(half, ku), upd_h[...], upd_l[...], NN)
        rh, rl = split2(residue)
        for j in range(ny):
            @pl.when(j <= y)
            def _():
                both_cores = mul(rh, inv_h[j], NN) + (mul(rh, inv_l[j], NN) + mul(rl, inv_h[j], NN))
                left, right = both_cores[:, :ks], both_cores[:, ks:]
                j_send[h, j] = jnp.where(c == 0, right, left)
                j_own[h, j] = jnp.where(c == 0, left, right)

            @pl.when(j > y)
            def _():
                j_send[h, j] = jnp.zeros_like(residue)
        send(j_send.at[h], j_pair.at[h], s_sem.at[10 + h], r_sem.at[11 + h], {"front": sib})

    def give_child(h):
        wait_recv(j_pair.at[h], r_sem.at[11 + h])
        for d in far_y:
            down = y >= d

            @pl.when(down)
            def _():
                at = (y + ny - d) % ny
                j_own[h, at] += j_pair[h, at]
                send(j_own.at[h, at], j_recv.at[h, d - 1], j_ss.at[h, d], j_rs.at[h, d], {"front": at * 2 + c})

        j_own[h, y] += j_pair[h, y]

    for h in range(2):
        sent(j_send.at[h], s_sem.at[10 + h])
        for d in far_y:
            sent(j_own.at[h, 0], j_ss.at[h, d], y >= d)

    def take_child(h):
        for d in near_y:
            up = y + d < ny

            @pl.when(up)
            def _():
                wait_recv(j_recv.at[h, d - 1], j_rs.at[h, d])
                j_own[h, y] += j_recv[h, d - 1]

        child_out[:, h] = j_own[h, y].reshape(ny, rows, ks)

    solve(0)
    give_update(0)
    solve(1)
    give_update(1)
    loads[4].wait()
    rinv_h[...], rinv_l[...] = split2(rinv_v[...])
    loads[5].wait()
    give_columns()

    @pl.when(c == 0)
    def _():
        give_reduced(0)

    @pl.when(c == 1)
    def _():
        give_reduced(1)

    give_forward(0)
    give_forward(1)
    give_solved(0)
    give_solved(1)
    give_backward(0)
    give_backward(1)
    give_root()

    @pl.when(c == 0)
    def _():
        give_picked(0)

    @pl.when(c == 1)
    def _():
        give_picked(1)

    take_picked(0)
    give_residue(0)
    give_child(0)
    take_picked(1)
    give_residue(1)
    give_child(1)
    take_child(0)
    take_child(1)
    finish()


def body(nl, nf, rhs_child, child_inverse, update_block, row_map, rhs_root, root_inverse):
    ny = nf // 2
    frames, ks = rhs_child.shape[1:]
    ku = update_block.shape[1]
    rows, width = rhs_root.shape
    deep = root_inverse.shape[0]
    half = ny * rows
    piece = half * deep // nl // rows
    nq = deep // piece
    vm = pltpu.VMEM
    dma = pltpu.SemaphoreType.DMA
    scratch = [
        vm((ny, 2, rows, ks), F32), vm((ks, nf * ks), F32), vm((ku, ks), F32), vm((deep, width), F32),
        vm((1, ku), jnp.int32), vm((rows, width), F32),
        vm((2, nf, ny, rows, ks), F32), vm((2, half, ks), F32),
        vm((ny, ks, 2 * ks), BF16), vm((ny, ks, 2 * ks), BF16),
        vm((ku, ks), BF16), vm((ku, ks), BF16),
        vm((deep, width), BF16), vm((deep, width), BF16),
        vm((width, ku), BF16),
        vm((ny, rows, ku), F32), vm((ny, rows, ku), F32), vm((ny, rows, ku), F32), vm((ny - 1, rows, ku), F32),
        vm((nl, rows, width), F32), vm((nl - 1, rows, width), F32),
        vm((2, ny, rows, width), F32),
        vm((2, nq, ny, rows, piece), F32), vm((2, nl - 1, rows, piece), F32),
        vm((2, nq, ny, rows, piece), F32),
        vm((2, ny, rows, width), F32), vm((nf, rows, width), F32),
        vm((nl, rows, width), F32),
        vm((2, ny, rows, ku), F32),
        vm((2, ny, half, ks), F32), vm((2, ny, half, ks), F32), vm((2, ny, half, ks), F32),
        vm((2, ny - 1, half, ks), F32),
        dma((6,)), dma((2, ny)), dma((2, ny)), dma((2, ny)), dma((2, ny)),
        dma((ny,)), dma((ny,)), dma((ny,)), dma((ny,)),
        dma((12,)), dma((13,)), dma((2, 2)), dma((2, ny)), dma((2, ny)),
    ]
    child, root = pl.pallas_call(
        functools.partial(kernel, nl, nf),
        out_shape=(
            jax.ShapeDtypeStruct((ny, 2, rows, ks), F32),
            jax.ShapeDtypeStruct((rows, width), F32),
        ),
        in_specs=[pl.BlockSpec(memory_space=pl.ANY)] * 6,
        out_specs=(pl.BlockSpec(memory_space=pltpu.VMEM),) * 2,
        scratch_shapes=scratch,
        compiler_params=pltpu.CompilerParams(
            collective_id=0, has_side_effects=True, vmem_limit_bytes=56 * 1024 * 1024
        ),
    )(
        rhs_child.reshape(ny, 2, rows, ks), child_inverse[0], update_block[0], row_map, rhs_root, root_inverse
    )
    return child.reshape(1, frames, ks), root


def solution(mesh):
    placed = (
        P("leaf", None, "front"),
        P("leaf", "front", None),
        P("leaf", None, "front"),
        P("leaf", None),
        P("front", "leaf"),
        P("front", "leaf"),
    )
    return jax.shard_map(
        functools.partial(body, mesh.shape["leaf"], mesh.shape["front"]),
        mesh=mesh,
        in_specs=placed,
        out_specs=(P("leaf", None, "front"), P("front", "leaf")),
        check_vma=False,
    )
```

```python
import functools

import jax
import jax.numpy as jnp
from jax import lax
from jax.experimental import pallas as pl
from jax.experimental.pallas import tpu as pltpu
from jax.sharding import PartitionSpec as P

NX = 4
MESH = pl.DeviceIdType.MESH
F32 = jnp.float32
BF16 = jnp.bfloat16
NN = (((1,), (0,)), ((), ()))
NT = (((1,), (1,)), ((), ()))


def split2(x):
    hi = x.astype(BF16)
    return hi, (x - hi.astype(F32)).astype(BF16)


def mul(a, b, dims):
    return lax.dot_general(a, b, dims, preferred_element_type=F32)


def mul3(a, bh, bl, dims):
    ah, al = split2(a)
    n = a.shape[0]
    both = mul(jnp.concatenate([ah, al], axis=0), bh, dims)
    return both[:n] + (both[n:] + mul(ah, bl, dims))


def ring_hops(d, n):
    return min(d, n - d)


def kernel(
    nl, nf,
    rhs_c, inv, upd, rmap, rhs_r, rinv,
    child_out, root_out,
    rhs_v, inv_v, upd_v, rinv_v, map_v, rr_v,
    gath, acc, inv_h, inv_l, upd_h, upd_l, rinv_h, rinv_l, onehot,
    b_send, b_recv, c_send, c_recv, d_buf, e_send, e_recv, f_buf,
    g_send, g_recv, h_buf, i_buf, j_send, j_recv,
    in_sem, p_ss, p_rs, a_ss, a_rs, s_sem, r_sem, j_ss, j_rs,
):
    ny = nf // 2
    nz = nl // NX
    l = lax.axis_index("leaf")
    f = lax.axis_index("front")
    y, c = f // 2, f % 2
    z, x = l // NX, l % NX
    sib = y * 2 + (1 - c)
    rows, width = rr_v.shape
    ks, ku = rhs_v.shape[-1], upd_v.shape[1]
    half = ny * rows
    nq = e_send.shape[0]

    far_y = sorted(range(1, ny), key=lambda d: -ring_hops(d, ny))
    near_y = sorted(range(1, ny), key=lambda d: ring_hops(d, ny))
    relayed_y = [d for d in (3, 4) if d < ny - 2]
    direct_y = [d for d in (2, 5, 6, 1, 7) if d < ny and d not in relayed_y] if ny > 4 else far_y
    arrive_y = [d for d in (2, 1, 7, 6, 5, 3, 4) if d < ny]
    far_l = sorted(
        [(dz, dx) for dz in range(nz) for dx in range(NX) if dz or dx],
        key=lambda d: -(ring_hops(d[0], nz) + ring_hops(d[1], NX)),
    )

    loads = [
        pltpu.make_async_copy(src, dst, in_sem.at[k])
        for k, (src, dst) in enumerate(
            [
                (rhs_c, rhs_v), (inv, inv_v.at[c]), (upd, upd_v.at[c]), (rmap, map_v),
                (rinv, rinv_v.at[c]), (rhs_r, rr_v),
            ]
        )
    ]
    for load in loads:
        load.start()
    barrier = pltpu.get_barrier_semaphore()
    for dz, dx in far_l:
        at = (z + dz) % nz * NX + (x + dx) % NX
        pl.semaphore_signal(barrier, inc=1, device_id={"leaf": at}, device_id_type=MESH)
    for d in far_y:
        for k in range(2):
            pl.semaphore_signal(barrier, inc=1, device_id={"front": (y + d) % ny * 2 + k}, device_id_type=MESH)
    pl.semaphore_signal(barrier, inc=1, device_id={"front": sib}, device_id_type=MESH)
    loads[0].wait()
    pl.semaphore_wait(barrier, nf + nl - 2)

    pending = []

    def send(src, dst, ss, rs, where):
        pltpu.make_async_remote_copy(
            src_ref=src, dst_ref=dst, send_sem=ss, recv_sem=rs, device_id=where, device_id_type=MESH
        ).start()

    def both(ref, sem):
        return pltpu.make_async_remote_copy(
            src_ref=ref, dst_ref=ref, send_sem=sem, recv_sem=sem, device_id={"front": sib}, device_id_type=MESH
        )

    def wait_recv(ref, sem):
        both(ref, sem).wait_recv()

    def sent(ref, sem, when=None):
        pending.append((ref, sem, when))

    def finish():
        for ref, sem, when in pending:
            if when is None:
                both(ref, sem).wait_send()
            else:
                @pl.when(when)
                def _():
                    both(ref, sem).wait_send()

    def on_leaf(k, src, dst, ref):
        for n, (dz, dx) in enumerate(far_l):
            at_z, at_x = (z + dz) % nz, (x + dx) % NX
            send(src(at_z, at_x), dst(n), s_sem.at[k], r_sem.at[k], {"leaf": at_z * NX + at_x})
        sent(ref, s_sem.at[k])

    def on_y(k, src, dst, ref):
        for n, d in enumerate(far_y):
            at = (y + d) % ny
            send(src(at), dst(n), s_sem.at[k], r_sem.at[k], {"front": at * 2 + c})
        sent(ref, s_sem.at[k])

    send(rhs_v.at[:, 1 - c], gath.at[f], p_ss.at[0], p_rs.at[0], {"front": sib})
    sent(rhs_v.at[:, 0], p_ss.at[0])
    for h in range(2):
        for d in direct_y:
            up = y + d < ny

            @pl.when(up)
            def _():
                send(rhs_v.at[:, h], gath.at[f], a_ss.at[h, d], a_rs.at[d], {"front": (y + d) % ny * 2 + h})

            sent(rhs_v.at[:, h], a_ss.at[h, d], up)
    for n, (src, dst) in enumerate([(inv, inv_v.at[c]), (upd, upd_v.at[c]), (rinv, rinv_v.at[c])]):
        send(src, dst, p_ss.at[n + 1], p_rs.at[n + 1], {"front": sib})
        sent(dst, p_ss.at[n + 1])
    gath[f] = rhs_v[:, c]

    loads[3].wait()
    low = map_v[...] % width
    onehot[...] = jnp.where(lax.broadcasted_iota(jnp.int32, (width, ku), 0) == low, 1.0, 0.0).astype(BF16)
    loads[1].wait()
    wait_recv(inv_v.at[0], p_rs.at[1])
    for j in range(ny):
        for k in range(2):
            inv_h[j, k * ks : (k + 1) * ks], inv_l[j, k * ks : (k + 1) * ks] = split2(
                inv_v[k, :, 2 * j * ks : 2 * (j + 1) * ks]
            )
    if relayed_y:
        @pl.when(y >= 2)
        def _():
            pair = gath.at[pl.ds((y + ny - 2) % ny * 2, 2)]
            wait_recv(pair, a_rs.at[2])
            for d in relayed_y:
                @pl.when(y + d - 2 < ny)
                def _():
                    send(pair, pair, a_ss.at[0, d], a_rs.at[d], {"front": (y + d - 2) % ny * 2 + c})

        for d in relayed_y:
            sent(gath.at[pl.ds(0, 2)], a_ss.at[0, d], (y >= 2) & (y + d - 2 < ny))
    loads[2].wait()
    wait_recv(upd_v.at[0], p_rs.at[2])
    for k in range(2):
        upd_h[:, k * ks : (k + 1) * ks], upd_l[:, k * ks : (k + 1) * ks] = split2(upd_v[k])

    def in_block():
        return lax.broadcasted_iota(jnp.int32, (nl, rows, ku), 0) == (map_v[...] // width)[None]

    def solve_step(at):
        pair = jnp.concatenate([gath[2 * at + k].reshape(half, ks) for k in range(2)], axis=1)
        return mul3(pair, inv_h[at], inv_l[at], NT)

    wait_recv(gath.at[0], p_rs.at[0])
    acc[...] = solve_step(y)
    for d in arrive_y:
        @pl.when(y >= d)
        def _():
            if d != 2 or not relayed_y:
                wait_recv(gath.at[pl.ds(0, 2)], a_rs.at[d])
            acc[...] += solve_step((y + ny - d) % ny)

    b_send[...] = mul3(acc[...], upd_h[...], upd_l[...], NT).reshape(ny, rows, ku)
    on_y(0, lambda at: b_send.at[at], lambda n: b_recv.at[n], b_recv)
    loads[4].wait()
    wait_recv(rinv_v.at[0], p_rs.at[3])
    deep = rinv_v.shape[1]
    for k in range(2):
        rinv_h[k * deep : (k + 1) * deep], rinv_l[k * deep : (k + 1) * deep] = split2(rinv_v[k])
    loads[5].wait()
    wait_recv(b_recv, r_sem.at[0])
    update = b_send[y] + jnp.sum(b_recv[...], axis=0)

    mask = in_block()
    parts = [
        jnp.where(mask, jnp.broadcast_to(p.astype(F32)[None], (nl, rows, ku)), 0.0).reshape(nl * rows, ku).astype(BF16)
        for p in split2(update)
    ]
    c_send[...] = (mul(parts[0], onehot[...], NT) + mul(parts[1], onehot[...], NT)).reshape(nl, rows, width)
    on_leaf(1, lambda at_z, at_x: c_send.at[at_z * NX + at_x], lambda n: c_recv.at[n], c_recv)
    wait_recv(c_recv, r_sem.at[1])

    d_buf[y] = rr_v[...] - (c_send[l] + jnp.sum(c_recv[...], axis=0))
    on_y(2, lambda at: d_buf.at[y], lambda n: d_buf.at[y], d_buf.at[pl.ds(0, ny - 1)])
    wait_recv(d_buf.at[pl.ds(0, ny - 1)], r_sem.at[2])

    part = mul3(d_buf[...].reshape(half, width), rinv_h[...], rinv_l[...], NT)
    piece = e_send.shape[-1]
    for q in range(nq):
        e_send[q] = part[:, q * piece : (q + 1) * piece].reshape(ny, rows, piece)
    on_leaf(3, lambda at_z, at_x: e_send.at[at_x, at_z], lambda n: e_recv.at[n], e_recv)
    wait_recv(e_recv, r_sem.at[3])
    f_buf[x, z] = e_send[x, z] + jnp.sum(e_recv[...], axis=0)

    on_leaf(4, lambda at_z, at_x: f_buf.at[x, z], lambda n: f_buf.at[x, z], e_recv)
    wait_recv(e_recv, r_sem.at[4])

    root = jnp.concatenate([f_buf[q].reshape(half, piece) for q in range(nq)], axis=1)
    g_send[...] = mul3(root, rinv_h[...], rinv_l[...], NN).reshape(ny, rows, width)
    on_y(5, lambda at: g_send.at[at], lambda n: g_recv.at[n], g_recv)
    wait_recv(g_recv, r_sem.at[5])
    answer = g_send[y] + jnp.sum(g_recv[...], axis=0)

    h_buf[l] = answer
    on_leaf(6, lambda at_z, at_x: h_buf.at[l], lambda n: h_buf.at[l], h_buf.at[pl.ds(0, nl - 1)])
    root_out[...] = answer
    wait_recv(h_buf.at[pl.ds(0, nl - 1)], r_sem.at[6])
    columns = jnp.concatenate(split2(h_buf[...].reshape(nl * rows, width)), axis=0)
    chosen = mul(columns, onehot[...], NN)
    chosen = (chosen[: nl * rows] + chosen[nl * rows :]).reshape(nl, rows, ku)

    i_buf[y] = jnp.sum(jnp.where(in_block(), chosen, 0.0), axis=0)
    on_y(7, lambda at: i_buf.at[y], lambda n: i_buf.at[y], i_buf.at[pl.ds(0, ny - 1)])
    wait_recv(i_buf.at[pl.ds(0, ny - 1)], r_sem.at[7])
    residue = acc[...] - mul3(i_buf[...].reshape(half, ku), upd_h[...], upd_l[...], NN)
    acc[...] = residue

    def back(d):
        at = (y + ny - d) % ny
        wide = mul3(acc[...], inv_h[at], inv_l[at], NN)
        for k in range(2):
            j_send[d, k] = wide[:, k * ks : (k + 1) * ks]
        return at

    for d in relayed_y[::-1]:
        @pl.when(y >= d)
        def _():
            back(d)
            send(j_send.at[d], j_recv.at[d], j_ss.at[d, 0], j_rs.at[d, 0], {"front": (y + ny + 2 - d) % ny * 2 + c})

        sent(j_send.at[0], j_ss.at[d, 0], y >= d)

    def give_child(d):
        down = y >= d

        @pl.when(down)
        def _():
            at = (y + ny - d) % ny
            for k in range(2):
                send(j_send.at[d, k], j_recv.at[d, c], j_ss.at[d, k], j_rs.at[d, c], {"front": at * 2 + k})

        for k in range(2):
            sent(j_send.at[0, 0], j_ss.at[d, k], down)

    for d in direct_y:
        @pl.when(y >= d)
        def _():
            back(d)

        if d != 2 or not relayed_y:
            give_child(d)
    if relayed_y:
        for d in relayed_y:
            @pl.when((y >= 2) & (y + d - 2 < ny))
            def _():
                wait_recv(j_recv.at[d], j_rs.at[d, 0])
                j_send[2] += j_recv[d]

        give_child(2)
    back(0)
    send(j_send.at[0, 1 - c], j_recv.at[0, c], j_ss.at[0, 0], j_rs.at[0, c], {"front": sib})
    sent(j_send.at[0, 0], j_ss.at[0, 0])
    j_recv[0, c] = j_send[0, c]
    wait_recv(j_recv.at[0, 0], j_rs.at[0, 1 - c])
    for d in arrive_y[1:] + arrive_y[:1]:
        if d in relayed_y:
            continue

        @pl.when(y + d < ny)
        def _():
            for h in range(2):
                wait_recv(j_recv.at[d, h], j_rs.at[d, h])
                j_recv[0, h] += j_recv[d, h]

    for h in range(2):
        child_out[:, h] = j_recv[0, h].reshape(ny, rows, ks)
    finish()


def body(nl, nf, rhs_child, child_inverse, update_block, row_map, rhs_root, root_inverse):
    ny = nf // 2
    frames, ks = rhs_child.shape[1:]
    ku = update_block.shape[1]
    rows, width = rhs_root.shape
    deep = root_inverse.shape[0]
    half = ny * rows
    piece = half * 2 * deep // nl // rows
    nq = 2 * deep // piece
    vm = pltpu.VMEM
    dma = pltpu.SemaphoreType.DMA
    scratch = [
        vm((ny, 2, rows, ks), F32), vm((2, ks, nf * ks), F32), vm((2, ku, ks), F32), vm((2, deep, width), F32),
        vm((1, ku), jnp.int32), vm((rows, width), F32),
        vm((nf, ny, rows, ks), F32), vm((half, 2 * ks), F32),
        vm((ny, 2 * ks, 2 * ks), BF16), vm((ny, 2 * ks, 2 * ks), BF16),
        vm((ku, 2 * ks), BF16), vm((ku, 2 * ks), BF16),
        vm((2 * deep, width), BF16), vm((2 * deep, width), BF16),
        vm((width, ku), BF16),
        vm((ny, rows, ku), F32), vm((ny - 1, rows, ku), F32),
        vm((nl, rows, width), F32), vm((nl - 1, rows, width), F32),
        vm((ny, rows, width), F32),
        vm((nq, ny, rows, piece), F32), vm((nl - 1, rows, piece), F32),
        vm((nq, ny, rows, piece), F32),
        vm((ny, rows, width), F32), vm((ny - 1, rows, width), F32),
        vm((nl, rows, width), F32),
        vm((ny, rows, ku), F32),
        vm((ny, 2, half, ks), F32), vm((ny, 2, half, ks), F32),
        dma((6,)), dma((4,)), dma((4,)), dma((2, ny)), dma((ny,)),
        dma((8,)), dma((8,)), dma((ny, 2)), dma((ny, 2)),
    ]
    child, root = pl.pallas_call(
        functools.partial(kernel, nl, nf),
        out_shape=(
            jax.ShapeDtypeStruct((ny, 2, rows, ks), F32),
            jax.ShapeDtypeStruct((rows, width), F32),
        ),
        in_specs=[pl.BlockSpec(memory_space=pl.ANY)] * 6,
        out_specs=(pl.BlockSpec(memory_space=pltpu.VMEM),) * 2,
        scratch_shapes=scratch,
        compiler_params=pltpu.CompilerParams(
            collective_id=0, has_side_effects=True, vmem_limit_bytes=56 * 1024 * 1024
        ),
    )(
        rhs_child.reshape(ny, 2, rows, ks), child_inverse[0], update_block[0], row_map, rhs_root, root_inverse
    )
    return child.reshape(1, frames, ks), root


def solution(mesh):
    placed = (
        P("leaf", None, "front"),
        P("leaf", "front", None),
        P("leaf", None, "front"),
        P("leaf", None),
        P("front", "leaf"),
        P("front", "leaf"),
    )
    return jax.shard_map(
        functools.partial(body, mesh.shape["leaf"], mesh.shape["front"]),
        mesh=mesh,
        in_specs=placed,
        out_specs=(P("leaf", None, "front"), P("front", "leaf")),
        check_vma=False,
    )
```

```python
import functools

import jax
import jax.numpy as jnp
from jax import lax
from jax.experimental import pallas as pl
from jax.experimental.pallas import tpu as pltpu
from jax.sharding import PartitionSpec as P

NX = 4
MESH = pl.DeviceIdType.MESH
F32 = jnp.float32
BF16 = jnp.bfloat16
NN = (((1,), (0,)), ((), ()))
NT = (((1,), (1,)), ((), ()))


def split2(x):
    hi = x.astype(BF16)
    return hi, (x - hi.astype(F32)).astype(BF16)


def mul(a, b, dims):
    return lax.dot_general(a, b, dims, preferred_element_type=F32)


def mul3(a, bh, bl, dims):
    ah, al = split2(a)
    n = a.shape[0]
    both = mul(jnp.concatenate([ah, al], axis=0), bh, dims)
    return both[:n] + (both[n:] + mul(ah, bl, dims))


def ring_hops(d, n):
    return min(d, n - d)


def kernel(
    nl, nf,
    rhs_c, inv, upd, rmap, rhs_r, rinv,
    child_out, root_out,
    rhs_v, inv_v, upd_v, rinv_v, map_v, rr_v,
    gath, acc, inv_h, inv_l, upd_h, upd_l, rinv_h, rinv_l, onehot,
    b_send, b_recv, c_send, c_recv, d_buf, e_send, e_recv, f_buf,
    g_send, g_recv, h_buf, i_buf, j_send, j_recv,
    in_sem, p_ss, p_rs, a_ss, a_rs, s_sem, r_sem, j_ss, j_rs,
):
    ny = nf // 2
    nz = nl // NX
    l = lax.axis_index("leaf")
    f = lax.axis_index("front")
    y, c = f // 2, f % 2
    z, x = l // NX, l % NX
    sib = y * 2 + (1 - c)
    rows, width = rr_v.shape
    ks, ku = rhs_v.shape[-1], upd_v.shape[1]
    half = ny * rows
    nq = e_send.shape[0]

    far_y = sorted(range(1, ny), key=lambda d: -ring_hops(d, ny))
    near_y = sorted(range(1, ny), key=lambda d: ring_hops(d, ny))
    relayed_y = [d for d in (3, 4) if d < ny - 2]
    direct_y = [d for d in (2, 5, 6, 1, 7) if d < ny and d not in relayed_y] if ny > 4 else far_y
    arrive_y = [d for d in (2, 1, 7, 6, 5, 3, 4) if d < ny]
    far_l = sorted(
        [(dz, dx) for dz in range(nz) for dx in range(NX) if dz or dx],
        key=lambda d: -(ring_hops(d[0], nz) + ring_hops(d[1], NX)),
    )

    loads = [
        pltpu.make_async_copy(src, dst, in_sem.at[k])
        for k, (src, dst) in enumerate(
            [
                (rhs_c, rhs_v), (inv, inv_v.at[c]), (upd, upd_v.at[c]), (rmap, map_v),
                (rinv, rinv_v.at[c]), (rhs_r, rr_v),
            ]
        )
    ]
    for load in loads:
        load.start()
    barrier = pltpu.get_barrier_semaphore()
    for dz, dx in far_l:
        at = (z + dz) % nz * NX + (x + dx) % NX
        pl.semaphore_signal(barrier, inc=1, device_id={"leaf": at}, device_id_type=MESH)
    for d in far_y:
        for k in range(2):
            pl.semaphore_signal(barrier, inc=1, device_id={"front": (y + d) % ny * 2 + k}, device_id_type=MESH)
    pl.semaphore_signal(barrier, inc=1, device_id={"front": sib}, device_id_type=MESH)
    loads[0].wait()
    pl.semaphore_wait(barrier, nf + nl - 2)

    pending = []

    def send(src, dst, ss, rs, where):
        pltpu.make_async_remote_copy(
            src_ref=src, dst_ref=dst, send_sem=ss, recv_sem=rs, device_id=where, device_id_type=MESH
        ).start()

    def both(ref, sem):
        return pltpu.make_async_remote_copy(
            src_ref=ref, dst_ref=ref, send_sem=sem, recv_sem=sem, device_id={"front": sib}, device_id_type=MESH
        )

    def wait_recv(ref, sem):
        both(ref, sem).wait_recv()

    def sent(ref, sem, when=None):
        pending.append((ref, sem, when))

    def finish():
        for ref, sem, when in pending:
            if when is None:
                both(ref, sem).wait_send()
            else:
                @pl.when(when)
                def _():
                    both(ref, sem).wait_send()

    def on_leaf(k, src, dst, ref):
        for n, (dz, dx) in enumerate(far_l):
            at_z, at_x = (z + dz) % nz, (x + dx) % NX
            send(src(at_z, at_x), dst(n), s_sem.at[k], r_sem.at[k], {"leaf": at_z * NX + at_x})
        sent(ref, s_sem.at[k])

    def by_column(k, make, src, dst):
        count = 0
        for dx in sorted(range(NX), key=lambda d: -ring_hops(d, NX)):
            at_x = (x + dx) % NX
            make(at_x)
            for dz in sorted(range(nz), key=lambda d: -ring_hops(d, nz)):
                if dz or dx:
                    at_z = (z + dz) % nz
                    send(
                        src.at[at_x, at_z], dst.at[count], s_sem.at[k], r_sem.at[k], {"leaf": at_z * NX + at_x}
                    )
                    count += 1
        sent(dst, s_sem.at[k])

    def on_y(k, src, dst, ref):
        for n, d in enumerate(far_y):
            at = (y + d) % ny
            send(src(at), dst(n), s_sem.at[k], r_sem.at[k], {"front": at * 2 + c})
        sent(ref, s_sem.at[k])

    send(rhs_v.at[:, 1 - c], gath.at[f], p_ss.at[0], p_rs.at[0], {"front": sib})
    sent(rhs_v.at[:, 0], p_ss.at[0])
    for h in range(2):
        for d in direct_y:
            up = y + d < ny

            @pl.when(up)
            def _():
                send(rhs_v.at[:, h], gath.at[f], a_ss.at[h, d], a_rs.at[d], {"front": (y + d) % ny * 2 + h})

            sent(rhs_v.at[:, h], a_ss.at[h, d], up)
    for n, (src, dst) in enumerate([(inv, inv_v.at[c]), (upd, upd_v.at[c]), (rinv, rinv_v.at[c])]):
        send(src, dst, p_ss.at[n + 1], p_rs.at[n + 1], {"front": sib})
        sent(dst, p_ss.at[n + 1])
    gath[f] = rhs_v[:, c]

    loads[3].wait()
    low = map_v[...] % width
    onehot[...] = jnp.where(lax.broadcasted_iota(jnp.int32, (width, ku), 0) == low, 1.0, 0.0).astype(BF16)
    loads[1].wait()
    wait_recv(inv_v.at[0], p_rs.at[1])
    for j in range(ny):
        for k in range(2):
            inv_h[j, k * ks : (k + 1) * ks], inv_l[j, k * ks : (k + 1) * ks] = split2(
                inv_v[k, :, 2 * j * ks : 2 * (j + 1) * ks]
            )
    if relayed_y:
        @pl.when(y >= 2)
        def _():
            pair = gath.at[pl.ds((y + ny - 2) % ny * 2, 2)]
            wait_recv(pair, a_rs.at[2])
            for d in relayed_y:
                @pl.when(y + d - 2 < ny)
                def _():
                    send(pair, pair, a_ss.at[0, d], a_rs.at[d], {"front": (y + d - 2) % ny * 2 + c})

        for d in relayed_y:
            sent(gath.at[pl.ds(0, 2)], a_ss.at[0, d], (y >= 2) & (y + d - 2 < ny))
    loads[2].wait()
    wait_recv(upd_v.at[0], p_rs.at[2])
    for k in range(2):
        upd_h[:, k * ks : (k + 1) * ks], upd_l[:, k * ks : (k + 1) * ks] = split2(upd_v[k])

    def in_block():
        return lax.broadcasted_iota(jnp.int32, (nl, rows, ku), 0) == (map_v[...] // width)[None]

    def solve_step(at):
        pair = jnp.concatenate([gath[2 * at + k].reshape(half, ks) for k in range(2)], axis=1)
        return mul3(pair, inv_h[at], inv_l[at], NT)

    wait_recv(gath.at[0], p_rs.at[0])
    acc[...] = solve_step(y)
    for d in arrive_y:
        @pl.when(y >= d)
        def _():
            if d != 2 or not relayed_y:
                wait_recv(gath.at[pl.ds(0, 2)], a_rs.at[d])
            acc[...] += solve_step((y + ny - d) % ny)

    b_send[...] = mul3(acc[...], upd_h[...], upd_l[...], NT).reshape(ny, rows, ku)
    on_y(0, lambda at: b_send.at[at], lambda n: b_recv.at[n], b_recv)
    loads[4].wait()
    wait_recv(rinv_v.at[0], p_rs.at[3])
    deep = rinv_v.shape[1]
    for k in range(2):
        rinv_h[k * deep : (k + 1) * deep], rinv_l[k * deep : (k + 1) * deep] = split2(rinv_v[k])
    loads[5].wait()
    wait_recv(b_recv, r_sem.at[0])
    update = b_send[y] + jnp.sum(b_recv[...], axis=0)

    high = map_v[...] // width
    values = [jnp.broadcast_to(p.astype(F32)[None], (nz, rows, ku)) for p in split2(update)]

    def spread(at_x):
        mask = lax.broadcasted_iota(jnp.int32, (nz, rows, ku), 0) * NX + at_x == high[None]
        placed = [jnp.where(mask, v, 0.0).reshape(nz * rows, ku).astype(BF16) for v in values]
        wide = mul(jnp.concatenate(placed, axis=0), onehot[...], NT)
        c_send[at_x] = (wide[: nz * rows] + wide[nz * rows :]).reshape(nz, rows, width)

    by_column(1, spread, c_send, c_recv)
    wait_recv(c_recv, r_sem.at[1])

    d_buf[y] = rr_v[...] - (c_send[x, z] + jnp.sum(c_recv[...], axis=0))
    on_y(2, lambda at: d_buf.at[y], lambda n: d_buf.at[y], d_buf.at[pl.ds(0, ny - 1)])
    wait_recv(d_buf.at[pl.ds(0, ny - 1)], r_sem.at[2])

    piece = e_send.shape[-1]
    ahead = d_buf[...].reshape(half, width)

    def forward(at_x):
        span = pl.ds(pl.multiple_of(at_x * piece, piece), piece)
        e_send[at_x] = mul3(ahead, rinv_h[span], rinv_l[span], NT).reshape(ny, rows, piece)

    by_column(3, forward, e_send, e_recv)
    wait_recv(e_recv, r_sem.at[3])
    f_buf[x, z] = e_send[x, z] + jnp.sum(e_recv[...], axis=0)

    on_leaf(4, lambda at_z, at_x: f_buf.at[x, z], lambda n: f_buf.at[x, z], e_recv)
    wait_recv(e_recv, r_sem.at[4])

    root = jnp.concatenate([f_buf[q].reshape(half, piece) for q in range(nq)], axis=1)
    g_send[...] = mul3(root, rinv_h[...], rinv_l[...], NN).reshape(ny, rows, width)
    on_y(5, lambda at: g_send.at[at], lambda n: g_recv.at[n], g_recv)
    wait_recv(g_recv, r_sem.at[5])
    answer = g_send[y] + jnp.sum(g_recv[...], axis=0)

    h_buf[l] = answer
    on_leaf(6, lambda at_z, at_x: h_buf.at[l], lambda n: h_buf.at[l], h_buf.at[pl.ds(0, nl - 1)])
    root_out[...] = answer
    wait_recv(h_buf.at[pl.ds(0, nl - 1)], r_sem.at[6])
    columns = jnp.concatenate(split2(h_buf[...].reshape(nl * rows, width)), axis=0)
    chosen = mul(columns, onehot[...], NN)
    chosen = (chosen[: nl * rows] + chosen[nl * rows :]).reshape(nl, rows, ku)

    i_buf[y] = jnp.sum(jnp.where(in_block(), chosen, 0.0), axis=0)
    on_y(7, lambda at: i_buf.at[y], lambda n: i_buf.at[y], i_buf.at[pl.ds(0, ny - 1)])
    wait_recv(i_buf.at[pl.ds(0, ny - 1)], r_sem.at[7])
    residue = acc[...] - mul3(i_buf[...].reshape(half, ku), upd_h[...], upd_l[...], NN)
    acc[...] = residue

    def back(d):
        at = (y + ny - d) % ny
        wide = mul3(acc[...], inv_h[at], inv_l[at], NN)
        for k in range(2):
            j_send[d, k] = wide[:, k * ks : (k + 1) * ks]
        return at

    for d in relayed_y[::-1]:
        @pl.when(y >= d)
        def _():
            back(d)
            send(j_send.at[d], j_recv.at[d], j_ss.at[d, 0], j_rs.at[d, 0], {"front": (y + ny + 2 - d) % ny * 2 + c})

        sent(j_send.at[0], j_ss.at[d, 0], y >= d)

    def give_child(d):
        down = y >= d

        @pl.when(down)
        def _():
            at = (y + ny - d) % ny
            for k in range(2):
                send(j_send.at[d, k], j_recv.at[d, c], j_ss.at[d, k], j_rs.at[d, c], {"front": at * 2 + k})

        for k in range(2):
            sent(j_send.at[0, 0], j_ss.at[d, k], down)

    for d in direct_y:
        @pl.when(y >= d)
        def _():
            back(d)

        if d != 2 or not relayed_y:
            give_child(d)
    if relayed_y:
        for d in relayed_y:
            @pl.when((y >= 2) & (y + d - 2 < ny))
            def _():
                wait_recv(j_recv.at[d], j_rs.at[d, 0])
                j_send[2] += j_recv[d]

        give_child(2)
    back(0)
    send(j_send.at[0, 1 - c], j_recv.at[0, c], j_ss.at[0, 0], j_rs.at[0, c], {"front": sib})
    sent(j_send.at[0, 0], j_ss.at[0, 0])
    j_recv[0, c] = j_send[0, c]
    wait_recv(j_recv.at[0, 0], j_rs.at[0, 1 - c])
    for d in arrive_y[1:] + arrive_y[:1]:
        if d in relayed_y:
            continue

        @pl.when(y + d < ny)
        def _():
            for h in range(2):
                wait_recv(j_recv.at[d, h], j_rs.at[d, h])
                j_recv[0, h] += j_recv[d, h]

    for h in range(2):
        child_out[:, h] = j_recv[0, h].reshape(ny, rows, ks)
    finish()


def body(nl, nf, rhs_child, child_inverse, update_block, row_map, rhs_root, root_inverse):
    ny = nf // 2
    frames, ks = rhs_child.shape[1:]
    ku = update_block.shape[1]
    rows, width = rhs_root.shape
    deep = root_inverse.shape[0]
    half = ny * rows
    piece = half * 2 * deep // nl // rows
    nq = 2 * deep // piece
    vm = pltpu.VMEM
    dma = pltpu.SemaphoreType.DMA
    scratch = [
        vm((ny, 2, rows, ks), F32), vm((2, ks, nf * ks), F32), vm((2, ku, ks), F32), vm((2, deep, width), F32),
        vm((1, ku), jnp.int32), vm((rows, width), F32),
        vm((nf, ny, rows, ks), F32), vm((half, 2 * ks), F32),
        vm((ny, 2 * ks, 2 * ks), BF16), vm((ny, 2 * ks, 2 * ks), BF16),
        vm((ku, 2 * ks), BF16), vm((ku, 2 * ks), BF16),
        vm((2 * deep, width), BF16), vm((2 * deep, width), BF16),
        vm((width, ku), BF16),
        vm((ny, rows, ku), F32), vm((ny - 1, rows, ku), F32),
        vm((NX, nl // NX, rows, width), F32), vm((nl - 1, rows, width), F32),
        vm((ny, rows, width), F32),
        vm((nq, ny, rows, piece), F32), vm((nl - 1, rows, piece), F32),
        vm((nq, ny, rows, piece), F32),
        vm((ny, rows, width), F32), vm((ny - 1, rows, width), F32),
        vm((nl, rows, width), F32),
        vm((ny, rows, ku), F32),
        vm((ny, 2, half, ks), F32), vm((ny, 2, half, ks), F32),
        dma((6,)), dma((4,)), dma((4,)), dma((2, ny)), dma((ny,)),
        dma((8,)), dma((8,)), dma((ny, 2)), dma((ny, 2)),
    ]
    child, root = pl.pallas_call(
        functools.partial(kernel, nl, nf),
        out_shape=(
            jax.ShapeDtypeStruct((ny, 2, rows, ks), F32),
            jax.ShapeDtypeStruct((rows, width), F32),
        ),
        in_specs=[pl.BlockSpec(memory_space=pl.ANY)] * 6,
        out_specs=(pl.BlockSpec(memory_space=pltpu.VMEM),) * 2,
        scratch_shapes=scratch,
        compiler_params=pltpu.CompilerParams(
            collective_id=0, has_side_effects=True, vmem_limit_bytes=56 * 1024 * 1024
        ),
    )(
        rhs_child.reshape(ny, 2, rows, ks), child_inverse[0], update_block[0], row_map, rhs_root, root_inverse
    )
    return child.reshape(1, frames, ks), root


def solution(mesh):
    placed = (
        P("leaf", None, "front"),
        P("leaf", "front", None),
        P("leaf", None, "front"),
        P("leaf", None),
        P("front", "leaf"),
        P("front", "leaf"),
    )
    return jax.shard_map(
        functools.partial(body, mesh.shape["leaf"], mesh.shape["front"]),
        mesh=mesh,
        in_specs=placed,
        out_specs=(P("leaf", None, "front"), P("front", "leaf")),
        check_vma=False,
    )
```

```python
import functools

import jax
import jax.numpy as jnp
from jax import lax
from jax.experimental import pallas as pl
from jax.experimental.pallas import tpu as pltpu
from jax.sharding import PartitionSpec as P

NX = 4
MESH = pl.DeviceIdType.MESH
F32 = jnp.float32
BF16 = jnp.bfloat16
NN = (((1,), (0,)), ((), ()))
NT = (((1,), (1,)), ((), ()))


def split2(x):
    hi = x.astype(BF16)
    return hi, (x - hi.astype(F32)).astype(BF16)


def mul(a, b, dims):
    return lax.dot_general(a, b, dims, preferred_element_type=F32)


def mul3(a, bh, bl, dims):
    ah, al = split2(a)
    n = a.shape[0]
    both = mul(jnp.concatenate([ah, al], axis=0), bh, dims)
    return both[:n] + (both[n:] + mul(ah, bl, dims))


def ring_hops(d, n):
    return min(d, n - d)


def kernel(
    nl, nf,
    rhs_c, inv, upd, rmap, rhs_r, rinv,
    child_out, root_out,
    rhs_v, inv_v, upd_v, rinv_v, map_v, rr_v,
    gath, acc, inv_h, inv_l, upd_h, upd_l, rinv_h, rinv_l, onehot,
    b_send, b_recv, c_send, c_recv, d_buf, e_send, e_recv, f_buf,
    g_send, g_recv, h_buf, i_buf, j_send, j_recv,
    in_sem, p_ss, p_rs, a_ss, a_rs, s_sem, r_sem, j_ss, j_rs,
):
    ny = nf // 2
    nz = nl // NX
    l = lax.axis_index("leaf")
    f = lax.axis_index("front")
    y, c = f // 2, f % 2
    z, x = l // NX, l % NX
    sib = y * 2 + (1 - c)
    rows, width = rr_v.shape
    ks, ku = rhs_v.shape[-1], upd_v.shape[1]
    half, kh = ny * rows, ku // 2
    nq = e_send.shape[0]

    far_y = sorted(range(1, ny), key=lambda d: -ring_hops(d, ny))
    near_y = sorted(range(1, ny), key=lambda d: ring_hops(d, ny))
    relayed_y = [d for d in (3, 4) if d < ny - 2]
    direct_y = [d for d in (2, 5, 6, 1, 7) if d < ny and d not in relayed_y] if ny > 4 else far_y
    arrive_y = [d for d in (2, 1, 7, 6, 5, 3, 4) if d < ny]
    far_l = sorted(
        [(dz, dx) for dz in range(nz) for dx in range(NX) if dz or dx],
        key=lambda d: -(ring_hops(d[0], nz) + ring_hops(d[1], NX)),
    )

    loads = [
        pltpu.make_async_copy(src, dst, in_sem.at[k])
        for k, (src, dst) in enumerate(
            [
                (rhs_c, rhs_v), (inv, inv_v.at[c]), (upd, upd_v.at[c]), (rmap, map_v),
                (rinv, rinv_v.at[c]), (rhs_r, rr_v),
            ]
        )
    ]
    for load in loads:
        load.start()
    barrier = pltpu.get_barrier_semaphore()
    for dz, dx in far_l:
        at = (z + dz) % nz * NX + (x + dx) % NX
        pl.semaphore_signal(barrier, inc=1, device_id={"leaf": at}, device_id_type=MESH)
    for d in far_y:
        for k in range(2):
            pl.semaphore_signal(barrier, inc=1, device_id={"front": (y + d) % ny * 2 + k}, device_id_type=MESH)
    pl.semaphore_signal(barrier, inc=1, device_id={"front": sib}, device_id_type=MESH)
    loads[0].wait()
    pl.semaphore_wait(barrier, nf + nl - 2)

    pending = []

    def send(src, dst, ss, rs, where):
        pltpu.make_async_remote_copy(
            src_ref=src, dst_ref=dst, send_sem=ss, recv_sem=rs, device_id=where, device_id_type=MESH
        ).start()

    def both(ref, sem):
        return pltpu.make_async_remote_copy(
            src_ref=ref, dst_ref=ref, send_sem=sem, recv_sem=sem, device_id={"front": sib}, device_id_type=MESH
        )

    def wait_recv(ref, sem):
        both(ref, sem).wait_recv()

    def sent(ref, sem, when=None):
        pending.append((ref, sem, when))

    def finish():
        for ref, sem, when in pending:
            if when is None:
                both(ref, sem).wait_send()
            else:
                @pl.when(when)
                def _():
                    both(ref, sem).wait_send()

    def on_leaf(k, src, dst, ref):
        for n, (dz, dx) in enumerate(far_l):
            at_z, at_x = (z + dz) % nz, (x + dx) % NX
            send(src(at_z, at_x), dst(n), s_sem.at[k], r_sem.at[k], {"leaf": at_z * NX + at_x})
        sent(ref, s_sem.at[k])

    def by_column(k, make, src, dst):
        count = 0
        for dx in sorted(range(NX), key=lambda d: -ring_hops(d, NX)):
            at_x = (x + dx) % NX
            make(at_x)
            for dz in sorted(range(nz), key=lambda d: -ring_hops(d, nz)):
                if dz or dx:
                    at_z = (z + dz) % nz
                    send(
                        src.at[at_x, at_z], dst.at[count], s_sem.at[k], r_sem.at[k], {"leaf": at_z * NX + at_x}
                    )
                    count += 1
        sent(dst, s_sem.at[k])

    def on_y(k, src, dst, ref):
        for n, d in enumerate(far_y):
            at = (y + d) % ny
            send(src(at), dst(n), s_sem.at[k], r_sem.at[k], {"front": at * 2 + c})
        sent(ref, s_sem.at[k])

    send(rhs_v.at[:, 1 - c], gath.at[f], p_ss.at[0], p_rs.at[0], {"front": sib})
    sent(rhs_v.at[:, 0], p_ss.at[0])
    for h in range(2):
        for d in direct_y:
            up = y + d < ny

            @pl.when(up)
            def _():
                send(rhs_v.at[:, h], gath.at[f], a_ss.at[h, d], a_rs.at[d], {"front": (y + d) % ny * 2 + h})

            sent(rhs_v.at[:, h], a_ss.at[h, d], up)
    for n, (src, dst) in enumerate([(inv, inv_v.at[c]), (upd, upd_v.at[c]), (rinv, rinv_v.at[c])]):
        send(src, dst, p_ss.at[n + 1], p_rs.at[n + 1], {"front": sib})
        sent(dst, p_ss.at[n + 1])
    gath[f] = rhs_v[:, c]

    loads[3].wait()
    low = map_v[...] % width
    onehot[...] = jnp.where(lax.broadcasted_iota(jnp.int32, (width, ku), 0) == low, 1.0, 0.0).astype(BF16)
    loads[1].wait()
    wait_recv(inv_v.at[0], p_rs.at[1])
    for j in range(ny):
        for k in range(2):
            inv_h[j, k * ks : (k + 1) * ks], inv_l[j, k * ks : (k + 1) * ks] = split2(
                inv_v[k, :, 2 * j * ks : 2 * (j + 1) * ks]
            )
    if relayed_y:
        @pl.when(y >= 2)
        def _():
            pair = gath.at[pl.ds((y + ny - 2) % ny * 2, 2)]
            wait_recv(pair, a_rs.at[2])
            for d in relayed_y:
                @pl.when(y + d - 2 < ny)
                def _():
                    send(pair, pair, a_ss.at[0, d], a_rs.at[d], {"front": (y + d - 2) % ny * 2 + c})

        for d in relayed_y:
            sent(gath.at[pl.ds(0, 2)], a_ss.at[0, d], (y >= 2) & (y + d - 2 < ny))
    loads[2].wait()
    wait_recv(upd_v.at[0], p_rs.at[2])
    for k in range(2):
        upd_h[:, k * ks : (k + 1) * ks], upd_l[:, k * ks : (k + 1) * ks] = split2(upd_v[k])

    def in_block(part):
        high = map_v[:, part] // width
        return lax.broadcasted_iota(jnp.int32, (nl, rows, high.shape[1]), 0) == high[None]

    def solve_step(at):
        pair = jnp.concatenate([gath[2 * at + k].reshape(half, ks) for k in range(2)], axis=1)
        return mul3(pair, inv_h[at], inv_l[at], NT)

    wait_recv(gath.at[0], p_rs.at[0])
    acc[...] = solve_step(y)
    for d in arrive_y:
        @pl.when(y >= d)
        def _():
            if d != 2 or not relayed_y:
                wait_recv(gath.at[pl.ds(0, 2)], a_rs.at[d])
            acc[...] += solve_step((y + ny - d) % ny)

    b_send[...] = mul3(acc[...], upd_h[...], upd_l[...], NT).reshape(ny, rows, ku)
    on_y(0, lambda at: b_send.at[at], lambda n: b_recv.at[n], b_recv)
    loads[4].wait()
    wait_recv(rinv_v.at[0], p_rs.at[3])
    deep = rinv_v.shape[1]
    for k in range(2):
        rinv_h[k * deep : (k + 1) * deep], rinv_l[k * deep : (k + 1) * deep] = split2(rinv_v[k])
    loads[5].wait()
    wait_recv(b_recv, r_sem.at[0])
    update = b_send[y] + jnp.sum(b_recv[...], axis=0)

    high = map_v[...] // width
    values = [jnp.broadcast_to(p.astype(F32)[None], (nz, rows, ku)) for p in split2(update)]

    def spread(at_x):
        mask = lax.broadcasted_iota(jnp.int32, (nz, rows, ku), 0) * NX + at_x == high[None]
        placed = [jnp.where(mask, v, 0.0).reshape(nz * rows, ku).astype(BF16) for v in values]
        wide = mul(jnp.concatenate(placed, axis=0), onehot[...], NT)
        c_send[at_x] = (wide[: nz * rows] + wide[nz * rows :]).reshape(nz, rows, width)

    by_column(1, spread, c_send, c_recv)
    wait_recv(c_recv, r_sem.at[1])

    d_buf[y] = rr_v[...] - (c_send[x, z] + jnp.sum(c_recv[...], axis=0))
    on_y(2, lambda at: d_buf.at[y], lambda n: d_buf.at[y], d_buf.at[pl.ds(0, ny - 1)])
    wait_recv(d_buf.at[pl.ds(0, ny - 1)], r_sem.at[2])

    piece = e_send.shape[-1]
    ahead = d_buf[...].reshape(half, width)

    def forward(at_x):
        span = pl.ds(pl.multiple_of(at_x * piece, piece), piece)
        e_send[at_x] = mul3(ahead, rinv_h[span], rinv_l[span], NT).reshape(ny, rows, piece)

    by_column(3, forward, e_send, e_recv)
    wait_recv(e_recv, r_sem.at[3])
    f_buf[x, z] = e_send[x, z] + jnp.sum(e_recv[...], axis=0)

    on_leaf(4, lambda at_z, at_x: f_buf.at[x, z], lambda n: f_buf.at[x, z], e_recv)
    wait_recv(e_recv, r_sem.at[4])

    root = jnp.concatenate([f_buf[q].reshape(half, piece) for q in range(nq)], axis=1)
    g_send[...] = mul3(root, rinv_h[...], rinv_l[...], NN).reshape(ny, rows, width)
    on_y(5, lambda at: g_send.at[at], lambda n: g_recv.at[n], g_recv)
    wait_recv(g_recv, r_sem.at[5])
    answer = g_send[y] + jnp.sum(g_recv[...], axis=0)

    h_buf[l] = answer
    on_leaf(6, lambda at_z, at_x: h_buf.at[l], lambda n: h_buf.at[l], h_buf.at[pl.ds(0, nl - 1)])
    root_out[...] = answer
    wait_recv(h_buf.at[pl.ds(0, nl - 1)], r_sem.at[6])
    columns = jnp.concatenate(split2(h_buf[...].reshape(nl * rows, width)), axis=0)

    for p in range(2):
        part = slice(p * kh, (p + 1) * kh)
        chosen = mul(columns, onehot[:, part], NN)
        chosen = (chosen[: nl * rows] + chosen[nl * rows :]).reshape(nl, rows, kh)
        i_buf[p, y] = jnp.sum(jnp.where(in_block(part), chosen, 0.0), axis=0)
        on_y(7 + p, lambda at: i_buf.at[p, y], lambda n: i_buf.at[p, y], i_buf.at[p, pl.ds(0, ny - 1)])
    residue = acc[...]
    for p in range(2):
        part = slice(p * kh, (p + 1) * kh)
        wait_recv(i_buf.at[p, pl.ds(0, ny - 1)], r_sem.at[7 + p])
        residue -= mul3(i_buf[p].reshape(half, kh), upd_h[part], upd_l[part], NN)
    acc[...] = residue

    def back(d):
        at = (y + ny - d) % ny
        wide = mul3(acc[...], inv_h[at], inv_l[at], NN)
        for k in range(2):
            j_send[d, k] = wide[:, k * ks : (k + 1) * ks]
        return at

    for d in relayed_y[::-1]:
        @pl.when(y >= d)
        def _():
            back(d)
            send(j_send.at[d], j_recv.at[d], j_ss.at[d, 0], j_rs.at[d, 0], {"front": (y + ny + 2 - d) % ny * 2 + c})

        sent(j_send.at[0], j_ss.at[d, 0], y >= d)

    def give_child(d):
        down = y >= d

        @pl.when(down)
        def _():
            at = (y + ny - d) % ny
            for k in range(2):
                send(j_send.at[d, k], j_recv.at[d, c], j_ss.at[d, k], j_rs.at[d, c], {"front": at * 2 + k})

        for k in range(2):
            sent(j_send.at[0, 0], j_ss.at[d, k], down)

    for d in direct_y:
        @pl.when(y >= d)
        def _():
            back(d)

        if d != 2 or not relayed_y:
            give_child(d)
    if relayed_y:
        for d in relayed_y:
            @pl.when((y >= 2) & (y + d - 2 < ny))
            def _():
                wait_recv(j_recv.at[d], j_rs.at[d, 0])
                j_send[2] += j_recv[d]

        give_child(2)
    back(0)
    send(j_send.at[0, 1 - c], j_recv.at[0, c], j_ss.at[0, 0], j_rs.at[0, c], {"front": sib})
    sent(j_send.at[0, 0], j_ss.at[0, 0])
    j_recv[0, c] = j_send[0, c]
    wait_recv(j_recv.at[0, 0], j_rs.at[0, 1 - c])
    for d in arrive_y[1:] + arrive_y[:1]:
        if d in relayed_y:
            continue

        @pl.when(y + d < ny)
        def _():
            for h in range(2):
                wait_recv(j_recv.at[d, h], j_rs.at[d, h])
                j_recv[0, h] += j_recv[d, h]

    for h in range(2):
        child_out[:, h] = j_recv[0, h].reshape(ny, rows, ks)
    finish()


def body(nl, nf, rhs_child, child_inverse, update_block, row_map, rhs_root, root_inverse):
    ny = nf // 2
    frames, ks = rhs_child.shape[1:]
    ku = update_block.shape[1]
    rows, width = rhs_root.shape
    deep = root_inverse.shape[0]
    half = ny * rows
    piece = half * 2 * deep // nl // rows
    nq = 2 * deep // piece
    vm = pltpu.VMEM
    dma = pltpu.SemaphoreType.DMA
    scratch = [
        vm((ny, 2, rows, ks), F32), vm((2, ks, nf * ks), F32), vm((2, ku, ks), F32), vm((2, deep, width), F32),
        vm((1, ku), jnp.int32), vm((rows, width), F32),
        vm((nf, ny, rows, ks), F32), vm((half, 2 * ks), F32),
        vm((ny, 2 * ks, 2 * ks), BF16), vm((ny, 2 * ks, 2 * ks), BF16),
        vm((ku, 2 * ks), BF16), vm((ku, 2 * ks), BF16),
        vm((2 * deep, width), BF16), vm((2 * deep, width), BF16),
        vm((width, ku), BF16),
        vm((ny, rows, ku), F32), vm((ny - 1, rows, ku), F32),
        vm((NX, nl // NX, rows, width), F32), vm((nl - 1, rows, width), F32),
        vm((ny, rows, width), F32),
        vm((nq, ny, rows, piece), F32), vm((nl - 1, rows, piece), F32),
        vm((nq, ny, rows, piece), F32),
        vm((ny, rows, width), F32), vm((ny - 1, rows, width), F32),
        vm((nl, rows, width), F32),
        vm((2, ny, rows, ku // 2), F32),
        vm((ny, 2, half, ks), F32), vm((ny, 2, half, ks), F32),
        dma((6,)), dma((4,)), dma((4,)), dma((2, ny)), dma((ny,)),
        dma((9,)), dma((9,)), dma((ny, 2)), dma((ny, 2)),
    ]
    child, root = pl.pallas_call(
        functools.partial(kernel, nl, nf),
        out_shape=(
            jax.ShapeDtypeStruct((ny, 2, rows, ks), F32),
            jax.ShapeDtypeStruct((rows, width), F32),
        ),
        in_specs=[pl.BlockSpec(memory_space=pl.ANY)] * 6,
        out_specs=(pl.BlockSpec(memory_space=pltpu.VMEM),) * 2,
        scratch_shapes=scratch,
        compiler_params=pltpu.CompilerParams(
            collective_id=0, has_side_effects=True, vmem_limit_bytes=56 * 1024 * 1024
        ),
    )(
        rhs_child.reshape(ny, 2, rows, ks), child_inverse[0], update_block[0], row_map, rhs_root, root_inverse
    )
    return child.reshape(1, frames, ks), root


def solution(mesh):
    placed = (
        P("leaf", None, "front"),
        P("leaf", "front", None),
        P("leaf", None, "front"),
        P("leaf", None),
        P("front", "leaf"),
        P("front", "leaf"),
    )
    return jax.shard_map(
        functools.partial(body, mesh.shape["leaf"], mesh.shape["front"]),
        mesh=mesh,
        in_specs=placed,
        out_specs=(P("leaf", None, "front"), P("front", "leaf")),
        check_vma=False,
    )
```
